32 devices in a mesh: groups: 2 (over y), length: 4 (over z), sector: 2 (over x), pair: 2 (over core).
Axes of the slice: x: 2, y: 2, z: 4, core: 2. Of those that a mesh axis runs over, the one named last changes fastest.
Arguments:
- flag_kernels: bfloat16 [4, 8, 32, 25, 1024], P('length', ('groups', 'sector', 'pair')), parts along dimension 1, may hold values from -1.1953125 to 1.1953125
- flag_unary: bfloat16 [4, 8, 32, 8, 1024], P('length', ('groups', 'sector', 'pair')), parts along dimension 1, may hold values from -8 to 8
- flag_labels: int32 [4, 8, 32, 1024], P('length', ('groups', 'sector', 'pair')), parts along dimension 1, may hold values from 0 to 7
- flag_mask: int32 [4, 8, 32, 1024], P('length', ('groups', 'sector', 'pair')), parts along dimension 1, may hold values 0 or 1
- dest_list: int32 [4, 8, 32], P('length', ('groups', 'sector', 'pair')), parts along dimension 1, may hold values from -1 to 3, as said below
- slot_list: int32 [4, 8, 32], P('length', ('groups', 'sector', 'pair')), parts along dimension 1, may hold values from -1 to 15, as said below
- res_kernels: bfloat16 [4, 8, 8, 25, 1024], P('length', ('groups', 'sector', 'pair')), parts along dimension 1, may hold values from -1.1953125 to 1.1953125
- res_unary: bfloat16 [4, 8, 8, 8, 1024], P('length', ('groups', 'sector', 'pair')), parts along dimension 1, may hold values from -8 to 8
- res_labels: int32 [4, 8, 8, 1024], P('length', ('groups', 'sector', 'pair')), parts along dimension 1, may hold values from 0 to 7
- res_mask: int32 [4, 8, 8, 1024], P('length', ('groups', 'sector', 'pair')), parts along dimension 1, may hold values 0 or 1
Outputs:
- flag_grad: bfloat16 [4, 8, 32, 25, 1024], P('length', ('groups', 'sector', 'pair')), parts along dimension 1
- res_grad: bfloat16 [4, 8, 8, 25, 1024], P('length', ('groups', 'sector', 'pair')), parts along dimension 1
- helper_loss: float32 [4, 8, 16], P('length', ('groups', 'sector', 'pair')), parts along dimension 1
The draws below stay inside these ranges and needn't reach their ends.
There are 2 independent parts, one for each index of `groups`. The reference program is written for one: setup_inputs(seed, part) draws one part's arguments, and reference() takes and returns one part's arrays. A program takes and returns all parts, laid end to end along the dimension named above; each array names one. Nothing has to cross between parts.
Inputs may be any that keep to these rules, and one draw needn't show every extreme that they name: `dest_list`: entry j of a device's list is -1 exactly when its slot j holds no flagged tile, and the -1 entries come after all others; at most 8 entries of one device name the same destination. `slot_list`: for each index along sector and pair, each pair of a destination along length and a slot 0 to 15 is named by exactly one entry of the lists of the devices along length; an entry is -1 exactly where dest_list is -1.
All inputs are finite; a program needn't handle non-finite values. No bound on the sum of `flag_mask` or of `res_mask` on one device may be relied on, other than what follows from the above.
Results may differ from the reference program's by a relative error of at most 0.001.
Values may be sent and summed in bfloat16 or wider, within the bound.
No kernel may reach another device: no remote copies, remote signals or barrier semaphores. Data moves between devices by JAX's collectives and lax.ppermute only.
A program may use at most 64 MiB of HBM per device.

```python
import jax
import jax.numpy as jnp
from jax import lax

CLASSES = 8
TAPS = 25
TILE = 32
ITERS = 3
FLAG_MAX = 32
RES = 8
PIX = 1024
NSP = 4
RECV = 16
N_LENGTH = 4
N_SECTOR = 2
N_PAIR = 2


def shuffle_slots(subkey):
    return jax.random.permutation(subkey, RECV)


def list_tables(key):
    device_count = N_LENGTH
    groups = N_SECTOR * N_PAIR

    def one_group(group_key):
        subkeys = jax.random.split(group_key, 6)
        spread = jax.random.randint(subkeys[0], (device_count // 2,), 0, RECV + 1)
        chosen = jax.random.randint(subkeys[1], (), 0, device_count // 2)
        spread = jnp.where(jnp.arange(device_count // 2) == chosen, RECV, spread)
        flip_sign = 2 * jax.random.randint(subkeys[2], (device_count // 2,), 0, 2) - 1
        paired = jnp.stack([RECV + flip_sign * spread, RECV - flip_sign * spread], axis=1).reshape(device_count)
        tile_loads = paired[jax.random.permutation(subkeys[3], device_count)]
        starts = jnp.cumsum(tile_loads) - tile_loads
        slot_order = jnp.arange(FLAG_MAX)
        global_index = starts[:, None] + slot_order[None, :]
        listed = slot_order[None, :] < tile_loads[:, None]
        rotation = jax.random.randint(subkeys[4], (), 0, device_count)
        target = (global_index + rotation) % device_count
        shuffles = jax.vmap(shuffle_slots)(jax.random.split(subkeys[5], device_count))
        slot_place = shuffles[target, jnp.minimum(global_index // device_count, RECV - 1)]
        return (jnp.where(listed, target, -1).astype(jnp.int32), jnp.where(listed, slot_place, -1).astype(jnp.int32))
    destinations, slot_names = jax.vmap(one_group)(jax.random.split(key, groups))
    return (jnp.transpose(destinations, (1, 0, 2)), jnp.transpose(slot_names, (1, 0, 2)))


def draw_dest_list(key, part):
    return list_tables(jax.random.fold_in(key, 11))[0]


def draw_slot_list(key, part):
    return list_tables(jax.random.fold_in(key, 11))[1]


def set_ends(array, own_key, low, high):
    shape = array.shape
    place = [jax.random.randint(jax.random.fold_in(own_key, axis), (), 0, shape[axis]) for axis in range(len(shape))]
    array = array.at[tuple(place)].set(low)
    longest = shape.index(max(shape))
    place[longest] = (place[longest] + 1) % shape[longest]
    return array.at[tuple(place)].set(high)


def block_levels(key, extent, cuts, least, top_value):
    gain, own = 1.0, jax.random.fold_in(key, 6)
    for dim, shards_of in cuts:
        draws = jnp.exp(jax.random.uniform(jax.random.fold_in(own, dim), (shards_of,), jnp.float32, least / len(cuts), top_value / len(cuts)))
        gain = gain * jnp.repeat(draws, extent[dim] // shards_of).reshape([-1 if axis == dim else 1 for axis in range(len(extent))])
    return gain


def gaussian(own_key, dims, width, bound, cuts=(), dtype=jnp.bfloat16):
    result = width * jax.random.normal(own_key, dims, jnp.float32)
    if cuts:
        result = result * block_levels(own_key, dims, cuts, -0.22, 0.18)
    return jnp.clip(result, -bound, bound).astype(dtype)


def setup_inputs(seed: int = 0, part: int = 0) -> dict:
    arg_keys = jax.random.split(jax.random.key(seed), 11)
    part_keys = jax.random.split(jax.random.fold_in(arg_keys[10], part), 11)
    flag_kernels = gaussian(part_keys[0], (N_LENGTH, NSP, FLAG_MAX, TAPS, PIX), 0.2, 1.1953125, ((0, 4), (1, 4)))
    flag_unary = gaussian(part_keys[1], (N_LENGTH, NSP, FLAG_MAX, CLASSES, PIX), 2.0, 8.0, ((0, 4), (1, 4)))
    flag_labels = set_ends(jax.random.randint(part_keys[2], (N_LENGTH, NSP, FLAG_MAX, PIX), 0, CLASSES), jax.random.fold_in(part_keys[2], 1), 0, CLASSES - 1).astype(jnp.int32)
    flag_mask = set_ends((jax.random.randint(part_keys[3], (N_LENGTH, NSP, FLAG_MAX, PIX), 0, 4) < 3).astype(jnp.int32), jax.random.fold_in(part_keys[3], 1), 0, 1)
    dest_list = draw_dest_list(jax.random.fold_in(jax.random.fold_in(arg_keys[10], part), 71), part)
    slot_list = draw_slot_list(jax.random.fold_in(jax.random.fold_in(arg_keys[10], part), 71), part)
    res_kernels = gaussian(part_keys[6], (N_LENGTH, NSP, RES, TAPS, PIX), 0.2, 1.1953125, ((0, 4), (1, 4)))
    res_unary = gaussian(part_keys[7], (N_LENGTH, NSP, RES, CLASSES, PIX), 2.0, 8.0, ((0, 4), (1, 4)))
    res_labels = set_ends(jax.random.randint(part_keys[8], (N_LENGTH, NSP, RES, PIX), 0, CLASSES), jax.random.fold_in(part_keys[8], 1), 0, CLASSES - 1).astype(jnp.int32)
    res_mask = set_ends((jax.random.randint(part_keys[9], (N_LENGTH, NSP, RES, PIX), 0, 4) < 3).astype(jnp.int32), jax.random.fold_in(part_keys[9], 1), 0, 1)
    return {"flag_kernels": flag_kernels, "flag_unary": flag_unary, "flag_labels": flag_labels, "flag_mask": flag_mask, "dest_list": dest_list, "slot_list": slot_list, "res_kernels": res_kernels, "res_unary": res_unary, "res_labels": res_labels, "res_mask": res_mask}


def normalize(logits):
    raised = jnp.exp(logits)
    return raised / lax.optimization_barrier(jnp.sum(raised, axis=0, keepdims=True))

def message(field_values, tap_weights):
    tile_side = TILE
    pixels = tile_side * tile_side
    margin = 2 * tile_side + 2
    padded = jnp.pad(field_values, ((0, 0), (margin, margin)))
    column = jnp.arange(pixels) % tile_side
    summed = jnp.zeros_like(field_values)
    tap_index = 0
    for row_step in range(-2, 3):
        for col_step in range(-2, 3):
            offset = row_step * tile_side + col_step
            shifted = lax.slice_in_dim(padded, margin + offset, margin + offset + pixels, axis=1)
            inside = ((column + col_step >= 0) & (column + col_step < tile_side)).astype(jnp.float32)
            summed = summed + (tap_weights[tap_index] * inside)[None, :] * shifted
            tap_index += 1
    return summed

def tile_objective(tap_weights, unary_terms, labels, weights):
    unary_terms = unary_terms.astype(jnp.float32)
    beliefs = normalize(unary_terms)
    logits = unary_terms
    for sweep_index in range(ITERS):
        logits = unary_terms + message(beliefs, tap_weights)
        if sweep_index + 1 < ITERS:
            beliefs = normalize(logits)
    summed = jnp.log(lax.optimization_barrier(jnp.sum(jnp.exp(logits), axis=0)))
    chosen = lax.optimization_barrier(jnp.sum(jnp.where(jnp.arange(CLASSES)[:, None] == labels[None, :], logits, 0.0), axis=0))
    return jnp.sum(weights * (summed - chosen))

def tile_work(tap_weights, unary_terms, labels, weights):
    total_value, gradient = jax.value_and_grad(tile_objective)(tap_weights.astype(jnp.float32), unary_terms, labels, weights)
    return (total_value / TILE, gradient.astype(jnp.bfloat16))

def batched(tap_weights, unary_terms, labels, weights, block_size):
    amount = tap_weights.shape[0]

    def compute_block(group_arrays):
        return jax.vmap(tile_work)(*group_arrays)
    shaped = tuple((member.reshape((amount // block_size, block_size) + member.shape[1:]) for member in (tap_weights, unary_terms, labels, weights)))
    losses, slopes = lax.map(compute_block, shaped)
    return (losses.reshape(amount), slopes.reshape((amount,) + slopes.shape[2:]))

def run_tiles(kernels, unary, labels, mask):
    leading = kernels.shape[:3]
    losses, slopes = batched(kernels.reshape((-1,) + kernels.shape[3:]), unary.reshape((-1,) + unary.shape[3:]), labels.reshape((-1, labels.shape[3])), mask.reshape((-1, mask.shape[3])).astype(jnp.float32), 16)
    return (losses.reshape(leading), slopes.reshape(kernels.shape))

def reference(flag_kernels, flag_unary, flag_labels, flag_mask, dest_list, slot_list, res_kernels, res_unary, res_labels, res_mask):
    flag_losses, flag_slopes = run_tiles(flag_kernels, flag_unary, flag_labels, flag_mask)
    resident_losses, resident_slopes = run_tiles(res_kernels, res_unary, res_labels, res_mask)
    is_listed = dest_list >= 0
    flag_grad = jnp.where(is_listed[..., None, None], flag_slopes, jnp.zeros_like(flag_slopes))
    leading = dest_list.shape
    row_index = jnp.where(is_listed, dest_list, N_LENGTH).astype(jnp.int32)
    columns = jnp.broadcast_to(jnp.arange(leading[1]).astype(jnp.int32)[None, :, None], leading)
    slot_index = jnp.where(is_listed, slot_list, 0).astype(jnp.int32)
    helper_loss = jnp.zeros((N_LENGTH, leading[1], RECV), jnp.float32).at[row_index, columns, slot_index].set(flag_losses, mode='drop')
    return (flag_grad, resident_slopes, helper_loss)
```

```python
import functools

import jax
import jax.numpy as jnp
from jax import lax
from jax.experimental import pallas as pl
from jax.experimental.pallas import tpu as pltpu
from jax.sharding import PartitionSpec as P

CLASSES = 8
DIFFS = CLASSES - 1
TAPS = 25
TILE = 32
ITERS = 3
RECV = 16
GROUP = 4
LANES = 128
PITCH = 40
TOP = 4
CHUNKS = 8
STEP = 4
F32 = jnp.float32


def unrolled(count, body):
    for index in range(count):
        body(index)


def looped(count, body):
    def step(index, carry):
        body(index)
        return carry

    lax.fori_loop(0, count, step, 0)


def swap_blocks(parts, lane):
    low_half = lane < 64
    even = (lane // TILE) % 2 == 0
    half = [None] * 4
    for j in (0, 1):
        half[j] = jnp.where(low_half, parts[j], pltpu.roll(parts[j + 2], 64, 1))
        half[j + 2] = jnp.where(low_half, pltpu.roll(parts[j], 64, 1), parts[j + 2])
    out = [None] * 4
    for j in (0, 2):
        out[j] = jnp.where(even, half[j], pltpu.roll(half[j + 1], TILE, 1))
        out[j + 1] = jnp.where(even, pltpu.roll(half[j], LANES - TILE, 1), half[j + 1])
    return out


def rows(base, phase):
    return pl.ds(base + phase, 8, stride=STEP)


def tile_kernel(flagged, ranks, *refs):
    if flagged:
        dest_ref, slot_ref, *refs = refs
    k_ref, u_ref, lab_ref, msk_ref, *refs = refs
    if flagged:
        out_ref, loss_ref, *refs = refs
    else:
        out_ref, *refs = refs
    kx, ux, lx, fields, beliefs, grads, acc, sums = refs
    group = pl.program_id(0)

    @pl.when(group == 0)
    def _():
        kx[...] = jnp.zeros_like(kx)
        fields[...] = jnp.zeros_like(fields)
        grads[...] = jnp.zeros_like(grads)
        if flagged:
            sums[...] = jnp.zeros_like(sums)

    def field_base(it, b, c):
        return ((it * 5 + b) * DIFFS + c) * PITCH + TOP

    def grad_base(it, c):
        return (it * DIFFS + c) * PITCH + TOP

    def work():
        lane25 = lax.broadcasted_iota(jnp.int32, (TAPS, LANES), 1)
        tap25 = lax.broadcasted_iota(jnp.int32, (TAPS, LANES), 0)
        seen = lane25 % TILE + tap25 % 5 - 2
        inside = ((seen >= 0) & (seen < TILE)).astype(F32)
        lane8 = lax.broadcasted_iota(jnp.int32, (8, LANES), 1)

        def bring(s):
            cut = pl.ds(s * LANES, LANES)
            parts = [k_ref[i, :, cut].astype(F32) for i in range(GROUP)]
            for r, value in enumerate(swap_blocks(parts, lane25)):
                kx[pl.ds(TOP + STEP * s + r, TAPS, stride=PITCH), :] = value * inside
            parts = [u_ref[i, :, cut].astype(F32) for i in range(GROUP)]
            for r, value in enumerate(swap_blocks(parts, lane8)):
                ux[pl.ds(STEP * s + r, CLASSES, stride=TILE), :] = value
            target = jnp.where(msk_ref[:, cut] == 1, lab_ref[:, cut], CLASSES)
            lx[pl.ds(s, 8, stride=8), :] = target

        unrolled(CHUNKS, bring)
        first = (group % 2) * GROUP
        labels = swap_blocks(
            [lx[pl.ds(pl.multiple_of(8 * (first + i), 8), 8), :] for i in range(GROUP)],
            lane8,
        )

        def spread(it, r, parts):
            for c, value in enumerate(parts):
                for b in range(5):
                    moved = value if b == 2 else pltpu.roll(value, (2 - b) % LANES, 1)
                    fields[rows(field_base(it, b, c), r), :] = moved

        def normalize(it, r, diffs):
            raised = [jnp.exp(d) for d in diffs]
            inverse = 1.0 / (functools.reduce(jnp.add, raised) + 1.0)
            spread(it, r, [(e - 1.0) * inverse for e in raised])
            if it > 0:
                for c in range(DIFFS):
                    beliefs[pl.ds(((it - 1) * DIFFS + c) * TILE + 8 * r, 8), :] = (
                        raised[c] * inverse
                    )

        for r in range(STEP):
            last = ux[pl.ds((CLASSES - 1) * TILE + r, 8, stride=STEP), :]
            diffs = [
                ux[pl.ds(c * TILE + r, 8, stride=STEP), :] - last for c in range(DIFFS)
            ]
            for c in range(DIFFS):
                ux[pl.ds(c * TILE + r, 8, stride=STEP), :] = diffs[c]
            normalize(0, r, diffs)

        for it in range(ITERS):
            for b in range(5):
                taps = [
                    [kx[rows((5 * a + b) * PITCH + TOP, r), :] for r in range(STEP)]
                    for a in range(5)
                ]
                for c in range(DIFFS):
                    near = [
                        fields[rows(field_base(it, b, c), r - 2), :] for r in range(8)
                    ]
                    for r in range(STEP):
                        place = pl.ds((c * STEP + r) * 8, 8)
                        if b == 0:
                            total = ux[pl.ds(c * TILE + r, 8, stride=STEP), :]
                        else:
                            total = acc[place, :]
                        for a in range(5):
                            total = total + taps[a][r] * near[r + a]
                        acc[place, :] = total
            if it + 1 < ITERS:
                for r in range(STEP):
                    normalize(
                        it + 1,
                        r,
                        [acc[pl.ds((c * STEP + r) * 8, 8), :] for c in range(DIFFS)],
                    )

        lost = jnp.zeros((8, LANES), F32)
        for r in range(STEP):
            diffs = [acc[pl.ds((c * STEP + r) * 8, 8), :] for c in range(DIFFS)]
            raised = [jnp.exp(d) for d in diffs]
            total = functools.reduce(jnp.add, raised) + 1.0
            inverse = 1.0 / total
            counted = labels[r] < CLASSES
            chosen = jnp.zeros((8, LANES), F32)
            for c in range(DIFFS):
                hit = labels[r] == c
                chosen = jnp.where(hit, diffs[c], chosen)
                slope = raised[c] * inverse - hit.astype(F32)
                grads[rows(grad_base(ITERS - 1, c), r), :] = jnp.where(
                    counted, slope, 0.0
                )
            lost = lost + jnp.where(counted, jnp.log(total) - chosen, 0.0)
        if flagged:
            sums[pl.ds(group, 1), :] = jnp.sum(lost, axis=0, keepdims=True)

        for it in range(ITERS - 1, 0, -1):
            for b in range(5):
                taps = [
                    [
                        kx[rows((5 * a + b) * PITCH + TOP, r - (a - 2)), :]
                        for r in range(STEP)
                    ]
                    for a in range(5)
                ]
                for c in range(DIFFS):
                    near = [
                        grads[rows(grad_base(it, c), r - 2), :] for r in range(8)
                    ]
                    for r in range(STEP):
                        place = pl.ds((c * STEP + r) * 8, 8)
                        total = taps[0][r] * near[r + 4]
                        for a in range(1, 5):
                            total = total + taps[a][r] * near[r + 4 - a]
                        if b != 2:
                            total = pltpu.roll(total, (b - 2) % LANES, 1)
                        if b > 0:
                            total = total + acc[place, :]
                        acc[place, :] = total
            for r in range(STEP):
                back = [acc[pl.ds((c * STEP + r) * 8, 8), :] for c in range(DIFFS)]
                mean = functools.reduce(
                    jnp.add,
                    [
                        back[c] * fields[rows(field_base(it, 2, c), r), :]
                        for c in range(DIFFS)
                    ],
                )
                for c in range(DIFFS):
                    belief = beliefs[pl.ds(((it - 1) * DIFFS + c) * TILE + 8 * r, 8), :]
                    grads[rows(grad_base(it - 1, c), r), :] = belief * (back[c] - mean)

        for b in range(5):
            totals = [[None] * STEP for _ in range(5)]
            for it in range(ITERS):
                for c in range(DIFFS):
                    near = [
                        fields[rows(field_base(it, b, c), r - 2), :] for r in range(8)
                    ]
                    for r in range(STEP):
                        slope = grads[rows(grad_base(it, c), r), :]
                        for a in range(5):
                            term = slope * near[r + a]
                            old = totals[a][r]
                            totals[a][r] = term if old is None else old + term
            for a in range(5):
                for r in range(STEP):
                    kx[rows((5 * a + b) * PITCH + TOP, r), :] = totals[a][r]

        def give(s):
            cut = pl.ds(s * LANES, LANES)
            parts = [
                kx[pl.ds(TOP + STEP * s + r, TAPS, stride=PITCH), :] * inside
                for r in range(STEP)
            ]
            for i, value in enumerate(swap_blocks(parts, lane25)):
                if flagged:
                    live = dest_ref[group * GROUP + i] >= 0
                    value = jnp.where(live, value, 0.0)
                out_ref[i, :, cut] = value.astype(jnp.bfloat16)

        unrolled(CHUNKS, give)

    if not flagged:
        work()
        return

    @pl.when(dest_ref[group * GROUP] >= 0)
    def _():
        work()

    @pl.when(dest_ref[group * GROUP] < 0)
    def _():
        out_ref[...] = jnp.zeros_like(out_ref)

    @pl.when(group == pl.num_programs(0) - 1)
    def _():
        lane = lax.broadcasted_iota(jnp.int32, sums.shape, 1)
        for i in range(GROUP):
            one = jnp.where(lane // TILE == i, sums[...], 0.0)
            one = jnp.sum(one, axis=1, keepdims=True) * (1.0 / TILE)
            acc[pl.ds(i * sums.shape[0], sums.shape[0]), :] = jnp.broadcast_to(
                one, sums.shape
            )
        spot = lax.broadcasted_iota(
            jnp.int32, (ranks, LANES), 0
        ) * LANES + lax.broadcasted_iota(jnp.int32, (ranks, LANES), 1)
        placed = jnp.zeros((ranks, LANES), F32)
        for j in range(sums.shape[0] * GROUP):
            here = dest_ref[j] * LANES + slot_ref[j]
            row = (j % GROUP) * sums.shape[0] + j // GROUP
            value = acc[pl.ds(row, 1), :]
            placed = jnp.where(spot == here, value, placed)
        loss_ref[...] = placed


def process(kernels, unary, labels, mask, lists, ranks):
    count = kernels.shape[0]
    steps = count // GROUP
    flagged = lists is not None

    def whole(*shape):
        return pl.BlockSpec(shape, lambda g, *_: (0,) * len(shape))

    def part(*shape):
        return pl.BlockSpec(shape, lambda g, *_: (g,) + (0,) * (len(shape) - 1))

    pixels = TILE * TILE
    out_shape = [jax.ShapeDtypeStruct(kernels.shape, jnp.bfloat16)]
    out_specs = [part(GROUP, TAPS, pixels)]
    if flagged:
        out_shape.append(jax.ShapeDtypeStruct((ranks, LANES), F32))
        out_specs.append(whole(ranks, LANES))
    return pl.pallas_call(
        functools.partial(tile_kernel, flagged, ranks),
        out_shape=out_shape,
        grid_spec=pltpu.PrefetchScalarGridSpec(
            num_scalar_prefetch=2 if flagged else 0,
            grid=(steps,),
            in_specs=[
                part(GROUP, TAPS, pixels),
                part(GROUP, CLASSES, pixels),
                pl.BlockSpec((8, pixels), lambda g, *_: (g // 2, 0)),
                pl.BlockSpec((8, pixels), lambda g, *_: (g // 2, 0)),
            ],
            out_specs=out_specs,
            scratch_shapes=[
                pltpu.VMEM((TAPS * PITCH, LANES), F32),
                pltpu.VMEM((CLASSES * TILE, LANES), F32),
                pltpu.VMEM((8 * 8, LANES), jnp.int32),
                pltpu.VMEM((ITERS * 5 * DIFFS * PITCH, LANES), F32),
                pltpu.VMEM(((ITERS - 1) * DIFFS * TILE, LANES), F32),
                pltpu.VMEM((ITERS * DIFFS * PITCH, LANES), F32),
                pltpu.VMEM((DIFFS * TILE, LANES), F32),
                pltpu.VMEM((max(8, steps), LANES), F32),
            ],
        ),
        compiler_params=pltpu.CompilerParams(vmem_limit_bytes=32 * 1024 * 1024),
        name="flag_tiles" if flagged else "res_tiles",
    )(*(lists if flagged else ()), kernels, unary, labels, mask)


def on_device(
    flag_kernels,
    flag_unary,
    flag_labels,
    flag_mask,
    dest_list,
    slot_list,
    res_kernels,
    res_unary,
    res_labels,
    res_mask,
):
    ranks = lax.axis_size("length")
    flag_grad, placed = process(
        flag_kernels[0, 0],
        flag_unary[0, 0],
        flag_labels[0, 0],
        flag_mask[0, 0],
        (dest_list[0, 0], slot_list[0, 0]),
        ranks,
    )
    got = lax.all_to_all(placed, "length", split_axis=0, concat_axis=0, tiled=True)
    (res_grad,) = process(
        res_kernels[0, 0], res_unary[0, 0], res_labels[0, 0], res_mask[0, 0], None, ranks
    )
    helper_loss = jnp.sum(got, axis=0)[:RECV]
    return flag_grad[None, None], res_grad[None, None], helper_loss[None, None]


def solution(mesh):
    tiles = ("groups", "sector", "pair")
    spec = lambda extra: P("length", tiles, *([None] * extra))
    in_specs = tuple(spec(n) for n in (3, 3, 2, 2, 1, 1, 3, 3, 2, 2))
    out_specs = tuple(spec(n) for n in (3, 3, 1))
    return jax.shard_map(
        on_device, mesh=mesh, in_specs=in_specs, out_specs=out_specs, check_vma=False
    )
```

```python
import functools

import jax
import jax.numpy as jnp
from jax import lax
from jax.experimental import pallas as pl
from jax.experimental.pallas import tpu as pltpu
from jax.sharding import PartitionSpec as P

CLASSES = 8
DIFFS = CLASSES - 1
TAPS = 25
TILE = 32
ITERS = 3
RECV = 16
LANES = 128
BLOCKS = 4
ROWS = 8
PIXELS = TILE * TILE
FIELD = ROWS * DIFFS * 8
PAIR = FIELD // 4
HALOED = 6 * PAIR
SPREAD = 5 * HALOED
SCORES = (CLASSES + 2) * 8
F32 = jnp.float32
BF16 = jnp.bfloat16


def dot(left, right):
    return jnp.dot(left, right, preferred_element_type=F32)


def tile_kernel(flagged, width, ranks, *refs):
    if flagged:
        dest_ref, slot_ref, me_ref, *refs = refs
    k_ref, u_ref, lab_ref, msk_ref, out_ref, *refs = refs
    if flagged:
        loss_refs, refs = refs[:ranks], refs[ranks:]
    swap, move, down, up, kx, kt, uu, ux, ud, acc, hl, fields, beliefs, grads, sums = refs
    block = pl.program_id(0)
    halves = width // 8

    @pl.when(block == 0)
    def _():
        row = lax.broadcasted_iota(jnp.int32, (LANES, LANES), 0)
        lane = lax.broadcasted_iota(jnp.int32, (LANES, LANES), 1)
        same = row % TILE == lane % TILE
        for j in range(BLOCKS):
            for r in range(BLOCKS):
                hit = same & (row // TILE == r) & (lane // TILE == j)
                swap[pl.ds(j * LANES, LANES), pl.ds(r * LANES, LANES)] = jnp.where(
                    hit, 1.0, 0.0
                ).astype(BF16)
        for b in range(5):
            seen = lane % TILE + b - 2
            inside = (seen >= 0) & (seen < TILE)
            for ref, jump in ((move, 0), (down, -TILE), (up, TILE)):
                place = b
                if jump == 0:
                    if b == 2:
                        continue
                    place = b - (b > 2)
                hit = inside & (row == lane + b - 2 + jump)
                part = jnp.where(hit, 1.0, 0.0).astype(BF16)
                for twice in range(2):
                    ref[pl.ds(twice * LANES, LANES), pl.ds(place * LANES, LANES)] = part
        uu[...] = jnp.zeros_like(uu)
        if flagged:
            sums[...] = jnp.zeros_like(sums)

    if flagged:
        live = jnp.int32(0)
        for j in range(sums.shape[0]):
            live = live + (dest_ref[j] >= 0).astype(jnp.int32)
    else:
        live = jnp.int32(width)
    active = jnp.clip((live - block * width + 7) // 8, 0, halves)

    def kernel_at(t, r):
        return ((r % 4) * 2 + r // 4) * TAPS + t

    def field_at(slot, b, r, c):
        return slot * SPREAD + ((b * 6 + (r + 2) // 2) * DIFFS + c) * 16 + (r % 2) * 8

    def plain_at(r, c):
        return ((r // 2) * DIFFS + c) * 16 + (r % 2) * 8

    def eight(start):
        return pl.ds(pl.multiple_of(start, 8), 8)

    def sixteen(start):
        return pl.ds(pl.multiple_of(start, 16), 16)

    def bring_kernels():
        for p in range(2):
            parts = []
            for j in range(BLOCKS):
                part = k_ref[:, :, pl.ds((2 * j + p) * LANES, LANES)]
                if width % 16:
                    part = part.astype(F32).reshape(TAPS * width, LANES).astype(BF16)
                else:
                    part = part.reshape(TAPS * width, LANES)
                parts.append(part)
            left = jnp.concatenate(parts, axis=1)
            for r in range(BLOCKS):
                got = dot(left, swap[:, pl.ds(r * LANES, LANES)])
                kx[pl.ds((r * 2 + p) * TAPS, TAPS), :, :] = got.reshape(
                    TAPS, width, LANES
                )

    def give_kernels():
        for p in range(2):
            left = jnp.concatenate(
                [
                    kx[pl.ds((r * 2 + p) * TAPS, TAPS), :, :]
                    .reshape(TAPS * width, LANES)
                    .astype(BF16)
                    for r in range(BLOCKS)
                ],
                axis=1,
            )
            for j in range(BLOCKS):
                got = dot(left, swap[:, pl.ds(j * LANES, LANES)])
                out_ref[:, :, pl.ds((2 * j + p) * LANES, LANES)] = got.reshape(
                    TAPS, width, LANES
                ).astype(BF16)

    def emit(slot, pair, c, value):
        fields[sixteen(field_at(slot, 2, 2 * pair, c)), :] = value
        high = value.astype(BF16)
        low = (value - high.astype(F32)).astype(BF16)
        place = pl.ds((pair * DIFFS + c) * 16, 16)
        hl[place, pl.ds(0, LANES)] = high
        hl[place, pl.ds(LANES, LANES)] = low

    def shift(slot):
        base = slot * SPREAD

        def put(b, pair, count, value):
            start = pl.multiple_of(base + (b * 6 + pair) * PAIR, 16)
            fields[pl.ds(start, count * PAIR), :] = value

        for n, b in enumerate((0, 1, 3, 4)):
            put(b, 1, 4, dot(hl[...], move[:, pl.ds(n * LANES, LANES)]))
        for b in range(5):
            cut = pl.ds(b * LANES, LANES)
            put(b, 0, 1, dot(hl[pl.ds(3 * PAIR, PAIR), :], down[:, cut]))
            put(b, 5, 1, dot(hl[pl.ds(0, PAIR), :], up[:, cut]))

    def message(taps_ref, mine, slot, start_ref):
        for b in range(5):
            for half in range(2):
                taps = [
                    [taps_ref[kernel_at(5 * a + b, 4 * half + r), mine, :] for r in range(4)]
                    for a in range(5)
                ]
                for c in range(DIFFS):
                    near = [
                        fields[eight(field_at(slot, b, 4 * half + r - 2, c)), :]
                        for r in range(8)
                    ]
                    for r in range(4):
                        place = pl.ds(plain_at(4 * half + r, c), 8)
                        if b == 0:
                            total = None if start_ref is None else start_ref[place, :]
                        else:
                            total = acc[place, :]
                        for a in range(5):
                            term = taps[a][r] * near[r + a]
                            total = term if total is None else total + term
                        acc[place, :] = total

    def work(h, carry):
        mine = pl.ds(pl.multiple_of(8 * h, 8), 8)

        for a in range(5):
            for b in range(5):
                for r in range(ROWS):
                    source = r - (a - 2)
                    turn = b - 2
                    if source < 0:
                        source, turn = source + ROWS, turn + TILE
                    elif source >= ROWS:
                        source, turn = source - ROWS, turn - TILE
                    value = kx[kernel_at(5 * a + b, source), mine, :]
                    if turn:
                        value = pltpu.roll(value, turn % LANES, 1)
                    kt[kernel_at(5 * (4 - a) + 4 - b, r), mine, :] = value

        index = block * width + 8 * h
        counted = lax.broadcasted_iota(jnp.int32, (8, LANES), 0) + index < live
        for s in range(8):
            cut = pl.ds(s * LANES, LANES)
            for i in range(8):
                uu[pl.ds(s * SCORES + i, CLASSES, stride=8), :] = u_ref[
                    8 * h + i, :, cut
                ].astype(F32)
            target = jnp.where(
                counted & (msk_ref[mine, cut] == 1), lab_ref[mine, cut], CLASSES
            )
            uu[pl.ds(s * SCORES + 8 * CLASSES, 8), :] = target.astype(F32)
        left = jnp.concatenate(
            [
                jnp.concatenate(
                    [
                        uu[pl.ds((2 * j + p) * SCORES, SCORES), :].astype(BF16)
                        for j in range(BLOCKS)
                    ],
                    axis=1,
                )
                for p in range(2)
            ],
            axis=0,
        )
        for r in range(BLOCKS):
            ux[pl.ds(r * 2 * SCORES, 2 * SCORES), :] = dot(
                left, swap[:, pl.ds(r * LANES, LANES)]
            )

        def score(r, f):
            return ux[pl.ds((r % 4) * 2 * SCORES + (r // 4) * SCORES + 8 * f, 8), :]

        for r in range(ROWS):
            last = score(r, CLASSES - 1)
            for c in range(DIFFS):
                value = score(r, c) - last
                ud[pl.ds(plain_at(r, c), 8), :] = value
                acc[pl.ds(plain_at(r, c), 8), :] = value

        def forward(it, carry):
            for pair in range(4):
                at = lambda c: pl.ds((pair * DIFFS + c) * 16, 16)
                raised = [jnp.exp(acc[at(c), :]) for c in range(DIFFS)]
                inverse = 1.0 / (functools.reduce(jnp.add, raised) + 1.0)
                for c in range(DIFFS):
                    belief = raised[c] * inverse
                    beliefs[sixteen(it * FIELD + (pair * DIFFS + c) * 16), :] = belief
                    emit(it, pair, c, belief - inverse)
            shift(it)
            message(kx, mine, it, ud)
            return carry

        lax.fori_loop(0, ITERS, forward, 0)

        lost = jnp.zeros((8, LANES), F32)
        for r in range(ROWS):
            label = score(r, CLASSES)
            diffs = [acc[pl.ds(plain_at(r, c), 8), :] for c in range(DIFFS)]
            raised = [jnp.exp(d) for d in diffs]
            total = functools.reduce(jnp.add, raised) + 1.0
            inverse = 1.0 / total
            used = label < CLASSES
            chosen = jnp.zeros((8, LANES), F32)
            for c in range(DIFFS):
                hit = label == c
                chosen = jnp.where(hit, diffs[c], chosen)
                slope = raised[c] * inverse - jnp.where(hit, 1.0, 0.0)
                grads[pl.ds((ITERS - 1) * FIELD + plain_at(r, c), 8), :] = jnp.where(
                    used, slope, 0.0
                )
            lost = lost + jnp.where(used, jnp.log(total) - chosen, 0.0)
        if flagged:
            lost = jnp.sum(lost, axis=1, keepdims=True) * (1.0 / TILE)
            sums[eight(index), :] = jnp.broadcast_to(lost, (8, LANES))

        def backward(step, carry):
            it = ITERS - 1 - step
            for pair in range(4):
                for c in range(DIFFS):
                    place = (pair * DIFFS + c) * 16
                    emit(ITERS, pair, c, grads[sixteen(it * FIELD + place), :])
            shift(ITERS)
            message(kt, mine, ITERS, None)
            for pair in range(4):
                at = lambda c: (pair * DIFFS + c) * 16
                back = [acc[pl.ds(at(c), 16), :] for c in range(DIFFS)]
                mean = functools.reduce(
                    jnp.add,
                    [
                        back[c] * fields[sixteen(field_at(it, 2, 2 * pair, c)), :]
                        for c in range(DIFFS)
                    ],
                )
                for c in range(DIFFS):
                    belief = beliefs[sixteen(it * FIELD + at(c)), :]
                    grads[sixteen((it - 1) * FIELD + at(c)), :] = belief * (back[c] - mean)
            return carry

        lax.fori_loop(0, ITERS - 1, backward, 0)

        for b in range(5):
            for half in range(2):
                totals = [[None] * 4 for _ in range(5)]
                for it in range(ITERS):
                    for c in range(DIFFS):
                        near = [
                            fields[pl.ds(field_at(it, b, 4 * half + r - 2, c), 8), :]
                            for r in range(8)
                        ]
                        for r in range(4):
                            slope = grads[
                                pl.ds(it * FIELD + plain_at(4 * half + r, c), 8), :
                            ]
                            for a in range(5):
                                term = slope * near[r + a]
                                old = totals[a][r]
                                totals[a][r] = term if old is None else old + term
                for a in range(5):
                    for r in range(4):
                        kx[kernel_at(5 * a + b, 4 * half + r), mine, :] = totals[a][r]
        return carry

    def zero(h, carry):
        mine = pl.ds(pl.multiple_of(8 * h, 8), 8)
        kx[:, mine, :] = jnp.zeros((kx.shape[0], 8, LANES), F32)
        return carry

    @pl.when(active > 0)
    def _():
        bring_kernels()
        lax.fori_loop(0, active, work, 0)
        if flagged:
            lax.fori_loop(active, halves, zero, 0)
        give_kernels()

    if not flagged:
        return

    @pl.when(active == 0)
    def _():
        out_ref[...] = jnp.zeros_like(out_ref)

    @pl.when(block == pl.num_programs(0) - 1)
    def _():
        high = -(-ranks // 8) * 8
        spot = lax.broadcasted_iota(
            jnp.int32, (high, LANES), 0
        ) * LANES + lax.broadcasted_iota(jnp.int32, (high, LANES), 1)
        placed = jnp.zeros((high, LANES), F32)
        for j in range(sums.shape[0]):
            far = dest_ref[j] - me_ref[0]
            far = jnp.where(far < 0, far + ranks, far)
            here = jnp.where(dest_ref[j] >= 0, far * LANES + slot_ref[j], -1)
            placed = jnp.where(spot == here, sums[pl.ds(j, 1), :], placed)
        for k, ref in enumerate(loss_refs):
            ref[...] = placed[k : k + 1, :]


def process(kernels, unary, labels, mask, lists, ranks):
    kernels = jnp.transpose(kernels, (1, 0, 2))
    count = kernels.shape[1]
    flagged = lists is not None
    width = 16 if count % 16 == 0 else 8

    out_shape = [jax.ShapeDtypeStruct(kernels.shape, BF16)]
    out_specs = [pl.BlockSpec((TAPS, width, PIXELS), lambda g, *_: (0, g, 0))]
    if flagged:
        out_shape += [jax.ShapeDtypeStruct((1, LANES), F32)] * ranks
        out_specs += [pl.BlockSpec((1, LANES), lambda g, *_: (0, 0))] * ranks
    grads, *rows = pl.pallas_call(
        functools.partial(tile_kernel, flagged, width, ranks),
        out_shape=out_shape,
        grid_spec=pltpu.PrefetchScalarGridSpec(
            num_scalar_prefetch=3 if flagged else 0,
            grid=(count // width,),
            in_specs=[
                pl.BlockSpec((TAPS, width, PIXELS), lambda g, *_: (0, g, 0)),
                pl.BlockSpec((width, CLASSES, PIXELS), lambda g, *_: (g, 0, 0)),
                pl.BlockSpec((width, PIXELS), lambda g, *_: (g, 0)),
                pl.BlockSpec((width, PIXELS), lambda g, *_: (g, 0)),
            ],
            out_specs=out_specs,
            scratch_shapes=[
                pltpu.VMEM((BLOCKS * LANES, BLOCKS * LANES), BF16),
                pltpu.VMEM((2 * LANES, 4 * LANES), BF16),
                pltpu.VMEM((2 * LANES, 5 * LANES), BF16),
                pltpu.VMEM((2 * LANES, 5 * LANES), BF16),
                pltpu.VMEM((ROWS * TAPS, width, LANES), F32),
                pltpu.VMEM((ROWS * TAPS, width, LANES), F32),
                pltpu.VMEM((8 * SCORES, LANES), F32),
                pltpu.VMEM((8 * SCORES, LANES), F32),
                pltpu.VMEM((FIELD, LANES), F32),
                pltpu.VMEM((FIELD, LANES), F32),
                pltpu.VMEM((FIELD, 2 * LANES), BF16),
                pltpu.VMEM(((ITERS + 1) * SPREAD, LANES), F32),
                pltpu.VMEM((ITERS * FIELD, LANES), F32),
                pltpu.VMEM((ITERS * FIELD, LANES), F32),
                pltpu.VMEM((count, LANES), F32),
            ],
        ),
        compiler_params=pltpu.CompilerParams(vmem_limit_bytes=40 * 1024 * 1024),
        name="flag_tiles" if flagged else "res_tiles",
    )(*(lists if flagged else ()), kernels, unary, labels, mask)
    return jnp.transpose(grads, (1, 0, 2)), rows


def on_device(
    flag_kernels,
    flag_unary,
    flag_labels,
    flag_mask,
    dest_list,
    slot_list,
    res_kernels,
    res_unary,
    res_labels,
    res_mask,
):
    ranks = lax.axis_size("length")
    me = lax.axis_index("length").astype(jnp.int32).reshape(1)
    flag_grad, rows = process(
        flag_kernels[0, 0],
        flag_unary[0, 0],
        flag_labels[0, 0],
        flag_mask[0, 0],
        (dest_list[0, 0], slot_list[0, 0], me),
        ranks,
    )
    got = [rows[0]] + [
        lax.ppermute(rows[k], "length", [(i, (i + k) % ranks) for i in range(ranks)])
        for k in range(1, ranks)
    ]
    res_grad, _ = process(
        res_kernels[0, 0], res_unary[0, 0], res_labels[0, 0], res_mask[0, 0], None, ranks
    )
    helper_loss = functools.reduce(jnp.add, got)[:, :RECV]
    return flag_grad[None, None], res_grad[None, None], helper_loss[None]


def solution(mesh):
    tiles = ("groups", "sector", "pair")
    spec = lambda extra: P("length", tiles, *([None] * extra))
    in_specs = tuple(spec(n) for n in (3, 3, 2, 2, 1, 1, 3, 3, 2, 2))
    out_specs = tuple(spec(n) for n in (3, 3, 1))
    return jax.shard_map(
        on_device, mesh=mesh, in_specs=in_specs, out_specs=out_specs, check_vma=False
    )
```

```python
import functools

import jax
import jax.numpy as jnp
from jax import lax
from jax.experimental import pallas as pl
from jax.experimental.pallas import tpu as pltpu
from jax.sharding import PartitionSpec as P

CLASSES = 8
DIFFS = CLASSES - 1
TAPS = 25
TILE = 32
ITERS = 3
RECV = 16
LANES = 128
BLOCKS = 4
PIXELS = TILE * TILE
PAIR = 2 * DIFFS * 8
SCORES = (CLASSES + 2) * 8
F32 = jnp.float32
BF16 = jnp.bfloat16


def dot(left, right):
    return jnp.dot(left, right, preferred_element_type=F32)


def tile_kernel(flagged, width, ranks, *refs):
    if flagged:
        dest_ref, slot_ref, me_ref, *refs = refs
    k_refs, refs = refs[:5], refs[5:]
    u_ref, lab_ref, msk_ref, out_ref, *refs = refs
    if flagged:
        loss_refs, refs = refs[:ranks], refs[ranks:]
    swap, move, down, up, kx, kt, uu, ux, ud, acc, hl, fields, beliefs, grads, sums = refs
    block = pl.program_id(0)
    teams = width // 8
    cuts = BLOCKS // teams
    rows = TILE // cuts
    quads = rows // 4
    field = rows // 2 * PAIR
    haloed = field + 2 * PAIR
    spread = 5 * haloed

    @pl.when(block == 0)
    def _():
        row = lax.broadcasted_iota(jnp.int32, (LANES, LANES), 0)
        lane = lax.broadcasted_iota(jnp.int32, (LANES, LANES), 1)
        same = row % TILE == lane % TILE
        for j in range(BLOCKS):
            for r in range(BLOCKS):
                hit = same & (row // TILE == r) & (lane // TILE == j)
                swap[pl.ds(j * LANES, LANES), pl.ds(r * LANES, LANES)] = jnp.where(
                    hit, 1.0, 0.0
                ).astype(BF16)
        for b in range(5):
            seen = lane % TILE + b - 2
            inside = (seen >= 0) & (seen < TILE)
            cut = lane // TILE % cuts
            for ref, jump in ((move, 0), (down, -TILE), (up, TILE)):
                place = b
                if jump == 0:
                    if b == 2:
                        continue
                    place = b - (b > 2)
                hit = inside & (row == lane + b - 2 + jump)
                if jump:
                    hit = hit & (cut > 0 if jump < 0 else cut < cuts - 1)
                part = jnp.where(hit, 1.0, 0.0).astype(BF16)
                for twice in range(2):
                    ref[pl.ds(twice * LANES, LANES), pl.ds(place * LANES, LANES)] = part
        for ref in (down, up):
            ref[:, pl.ds(5 * LANES, LANES)] = jnp.zeros((2 * LANES, LANES), BF16)
        uu[...] = jnp.zeros_like(uu)
        if flagged:
            sums[...] = jnp.zeros_like(sums)

    if flagged:
        live = jnp.int32(0)
        for j in range(sums.shape[0]):
            live = live + (dest_ref[j] >= 0).astype(jnp.int32)
    else:
        live = jnp.int32(width)

    def kernel_at(t, r):
        return ((r % 4) * quads + r // 4) * TAPS + t

    def field_at(slot, b, r, c):
        place = b * haloed + ((r + 2) // 2) * PAIR + c * 16 + (r % 2) * 8
        return slot * spread + place

    def plain_at(r, c):
        return ((r // 2) * DIFFS + c) * 16 + (r % 2) * 8

    def eight(start):
        return pl.ds(pl.multiple_of(start, 8), 8)

    def sixteen(start):
        return pl.ds(pl.multiple_of(start, 16), 16)

    def swapped(left):
        for two in range(BLOCKS // 2):
            got = dot(left, swap[:, pl.ds(two * 2 * LANES, 2 * LANES)])
            yield 2 * two, got[:, :LANES]
            yield 2 * two + 1, got[:, LANES:]

    def bring_kernels():
        for m in range(quads):
            parts = []
            for j in range(BLOCKS):
                team, cut = divmod(j, cuts)
                lanes = pl.ds((m + quads * cut) * LANES, LANES)
                part = jnp.concatenate([ref[:, :, lanes] for ref in k_refs], axis=0)
                part = part.astype(F32)[:, 8 * team : 8 * team + 8]
                parts.append(part.reshape(TAPS * 8, LANES).astype(BF16))
            for r, got in swapped(jnp.concatenate(parts, axis=1)):
                kx[pl.ds((r * quads + m) * TAPS, TAPS), :, :] = got.reshape(
                    TAPS, 8, LANES
                )

    def give_kernels():
        for m in range(quads):
            left = jnp.concatenate(
                [
                    kx[pl.ds((r * quads + m) * TAPS, TAPS), :, :]
                    .reshape(TAPS * 8, LANES)
                    .astype(BF16)
                    for r in range(BLOCKS)
                ],
                axis=1,
            )
            got = {j: part.reshape(TAPS, 8, LANES) for j, part in swapped(left)}
            for cut in range(cuts):
                part = [got[team * cuts + cut] for team in range(teams)]
                lanes = pl.ds((m + quads * cut) * LANES, LANES)
                out_ref[:, :, lanes] = jnp.concatenate(part, axis=1).astype(BF16)

    def emit(slot, pair, c, value):
        fields[sixteen(field_at(slot, 2, 2 * pair, c)), :] = value
        high = value.astype(BF16)
        low = (value - high.astype(F32)).astype(BF16)
        place = pl.ds(plain_at(2 * pair, c), 16)
        hl[place, pl.ds(0, LANES)] = high
        hl[place, pl.ds(LANES, LANES)] = low

    def shift(slot):
        def put(pair, source, matrix, names):
            got = dot(hl[source, :], matrix)
            for n, b in enumerate(names):
                start = field_at(slot, b, 2 * pair, 0)
                fields[pl.ds(pl.multiple_of(start, 16), source.size), :] = got[
                    :, n * LANES : (n + 1) * LANES
                ]

        first, last = pl.ds(0, PAIR), pl.ds(field - PAIR, PAIR)
        for two, names in enumerate(((2, 3), (0, 1), (4,))):
            lanes = pl.ds(names[0] * LANES, 2 * LANES)
            put(-1, last, down[:, lanes], names)
            put(rows // 2, first, up[:, lanes], names)
            if two == 0:
                put(0, pl.ds(0, field), move[:, pl.ds(0, 2 * LANES)], (0, 1))
            elif two == 1:
                put(0, pl.ds(0, field), move[:, pl.ds(2 * LANES, 2 * LANES)], (3, 4))

    def message(taps_ref, slot, start_ref):
        for b in (2, 0, 1, 3, 4):
            for quad in range(quads):
                taps = [
                    [taps_ref[kernel_at(5 * a + b, 4 * quad + r)] for r in range(4)]
                    for a in range(5)
                ]
                for c in range(DIFFS):
                    near = [
                        fields[eight(field_at(slot, b, 4 * quad + r - 2, c)), :]
                        for r in range(8)
                    ]
                    for r in range(4):
                        place = pl.ds(plain_at(4 * quad + r, c), 8)
                        if b == 2:
                            total = None if start_ref is None else start_ref[place, :]
                        else:
                            total = acc[place, :]
                        for a in range(5):
                            term = taps[a][r] * near[r + a]
                            total = term if total is None else total + term
                        acc[place, :] = total

    def work():
        for a in range(5):
            for b in range(5):
                for r in range(rows):
                    source = r - (a - 2)
                    turn = b - 2
                    if source < 0:
                        source, turn = source + rows, turn + TILE
                    elif source >= rows:
                        source, turn = source - rows, turn - TILE
                    value = kx[kernel_at(5 * a + b, source)]
                    if turn:
                        value = pltpu.roll(value, turn % LANES, 1)
                    kt[kernel_at(5 * (4 - a) + 4 - b, r)] = value

        index = lax.broadcasted_iota(jnp.int32, (8, LANES), 0) + block * width
        for team in range(teams):
            mine = pl.ds(8 * team, 8)
            for s in range(8):
                cut = pl.ds(s * LANES, LANES)
                for i in range(8):
                    uu[team, pl.ds(s * SCORES + i, CLASSES, stride=8), :] = u_ref[
                        8 * team + i, :, cut
                    ].astype(F32)
                target = jnp.where(
                    (index + 8 * team < live) & (msk_ref[mine, cut] == 1),
                    lab_ref[mine, cut],
                    CLASSES,
                )
                uu[team, pl.ds(s * SCORES + 8 * CLASSES, 8), :] = target.astype(F32)
        left = jnp.concatenate(
            [
                jnp.concatenate(
                    [
                        uu[
                            j // cuts, pl.ds((m + quads * (j % cuts)) * SCORES, SCORES), :
                        ].astype(BF16)
                        for j in range(BLOCKS)
                    ],
                    axis=1,
                )
                for m in range(quads)
            ],
            axis=0,
        )
        for r, got in swapped(left):
            ux[pl.ds(r * quads * SCORES, quads * SCORES), :] = got

        def score(r, f):
            return ux[pl.ds(((r % 4) * quads + r // 4) * SCORES + 8 * f, 8), :]

        for r in range(rows):
            last = score(r, CLASSES - 1)
            for c in range(DIFFS):
                value = score(r, c) - last
                ud[pl.ds(plain_at(r, c), 8), :] = value
                acc[pl.ds(plain_at(r, c), 8), :] = value

        def forward(it, carry):
            for pair in range(rows // 2):
                at = lambda c: pl.ds(plain_at(2 * pair, c), 16)
                raised = [jnp.exp(acc[at(c), :]) for c in range(DIFFS)]
                inverse = 1.0 / (functools.reduce(jnp.add, raised) + 1.0)
                for c in range(DIFFS):
                    belief = raised[c] * inverse
                    beliefs[sixteen(it * field + plain_at(2 * pair, c)), :] = belief
                    emit(it, pair, c, belief - inverse)
            shift(it)
            message(kx, it, ud)
            return carry

        lax.fori_loop(0, ITERS, forward, 0)

        lost = jnp.zeros((8, LANES), F32)
        for r in range(rows):
            label = score(r, CLASSES)
            diffs = [acc[pl.ds(plain_at(r, c), 8), :] for c in range(DIFFS)]
            raised = [jnp.exp(d) for d in diffs]
            total = functools.reduce(jnp.add, raised) + 1.0
            inverse = 1.0 / total
            used = label < CLASSES
            chosen = jnp.zeros((8, LANES), F32)
            for c in range(DIFFS):
                hit = label == c
                chosen = jnp.where(hit, diffs[c], chosen)
                slope = raised[c] * inverse - jnp.where(hit, 1.0, 0.0)
                grads[pl.ds((ITERS - 1) * field + plain_at(r, c), 8), :] = jnp.where(
                    used, slope, 0.0
                )
            lost = lost + jnp.where(used, jnp.log(total) - chosen, 0.0)
        if flagged:
            lane = lax.broadcasted_iota(jnp.int32, (8, LANES), 1)
            for team in range(teams):
                one = jnp.where(lane // (cuts * TILE) == team, lost, 0.0)
                one = jnp.sum(one, axis=1, keepdims=True) * (1.0 / TILE)
                sums[eight(block * width + 8 * team), :] = jnp.broadcast_to(one, (8, LANES))

        def backward(step, carry):
            it = ITERS - 1 - step
            for pair in range(rows // 2):
                for c in range(DIFFS):
                    place = plain_at(2 * pair, c)
                    emit(ITERS, pair, c, grads[sixteen(it * field + place), :])
            shift(ITERS)
            message(kt, ITERS, None)
            for pair in range(rows // 2):
                at = lambda c: plain_at(2 * pair, c)
                back = [acc[pl.ds(at(c), 16), :] for c in range(DIFFS)]
                mean = functools.reduce(
                    jnp.add,
                    [
                        back[c] * fields[sixteen(field_at(it, 2, 2 * pair, c)), :]
                        for c in range(DIFFS)
                    ],
                )
                for c in range(DIFFS):
                    belief = beliefs[sixteen(it * field + at(c)), :]
                    grads[sixteen((it - 1) * field + at(c)), :] = belief * (back[c] - mean)
            return carry

        lax.fori_loop(0, ITERS - 1, backward, 0)

        def gather(b, carry):
            for quad in range(quads):
                totals = [[None] * 4 for _ in range(5)]
                for it in range(ITERS):
                    for c in range(DIFFS):
                        near = [
                            fields[eight(field_at(it, b, 4 * quad + r - 2, c)), :]
                            for r in range(8)
                        ]
                        for r in range(4):
                            slope = grads[
                                pl.ds(it * field + plain_at(4 * quad + r, c), 8), :
                            ]
                            for a in range(5):
                                term = slope * near[r + a]
                                old = totals[a][r]
                                totals[a][r] = term if old is None else old + term
                for a in range(5):
                    for r in range(4):
                        kx[kernel_at(5 * a + b, 4 * quad + r)] = totals[a][r]
            return carry

        lax.fori_loop(0, 5, gather, 0)

    @pl.when(live > block * width)
    def _():
        bring_kernels()
        work()
        give_kernels()

    if not flagged:
        return

    @pl.when(live <= block * width)
    def _():
        out_ref[...] = jnp.zeros_like(out_ref)

    @pl.when(block == pl.num_programs(0) - 1)
    def _():
        high = -(-ranks // 8) * 8
        spot = lax.broadcasted_iota(
            jnp.int32, (high, LANES), 0
        ) * LANES + lax.broadcasted_iota(jnp.int32, (high, LANES), 1)
        placed = jnp.zeros((high, LANES), F32)
        for j in range(sums.shape[0]):
            far = dest_ref[j] - me_ref[0]
            far = jnp.where(far < 0, far + ranks, far)
            here = jnp.where(dest_ref[j] >= 0, far * LANES + slot_ref[j], -1)
            placed = jnp.where(spot == here, sums[pl.ds(j, 1), :], placed)
        for k, ref in enumerate(loss_refs):
            ref[...] = placed[k : k + 1, :]


def process(kernels, unary, labels, mask, lists, ranks):
    kernels = jnp.transpose(kernels, (1, 0, 2))
    count = kernels.shape[1]
    flagged = lists is not None
    width = 16 if count % 16 == 0 else 8
    rows = TILE * width // (8 * BLOCKS)
    field = rows // 2 * PAIR
    haloed = field + 2 * PAIR

    out_shape = [jax.ShapeDtypeStruct(kernels.shape, BF16)]
    out_specs = [pl.BlockSpec((TAPS, width, PIXELS), lambda g, *_: (0, g, 0))]
    if flagged:
        out_shape += [jax.ShapeDtypeStruct((1, LANES), F32)] * ranks
        out_specs += [pl.BlockSpec((1, LANES), lambda g, *_: (0, 0))] * ranks
    grads, *rows = pl.pallas_call(
        functools.partial(tile_kernel, flagged, width, ranks),
        out_shape=out_shape,
        grid_spec=pltpu.PrefetchScalarGridSpec(
            num_scalar_prefetch=3 if flagged else 0,
            grid=(count // width,),
            in_specs=[
                *[
                    pl.BlockSpec((5, width, PIXELS), lambda g, *_, a=a: (a, g, 0))
                    for a in range(5)
                ],
                pl.BlockSpec((width, CLASSES, PIXELS), lambda g, *_: (g, 0, 0)),
                pl.BlockSpec((width, PIXELS), lambda g, *_: (g, 0)),
                pl.BlockSpec((width, PIXELS), lambda g, *_: (g, 0)),
            ],
            out_specs=out_specs,
            scratch_shapes=[
                pltpu.VMEM((BLOCKS * LANES, BLOCKS * LANES), BF16),
                pltpu.VMEM((2 * LANES, 4 * LANES), BF16),
                pltpu.VMEM((2 * LANES, 6 * LANES), BF16),
                pltpu.VMEM((2 * LANES, 6 * LANES), BF16),
                pltpu.VMEM((rows * TAPS, 8, LANES), F32),
                pltpu.VMEM((rows * TAPS, 8, LANES), F32),
                pltpu.VMEM((width // 8, 8 * SCORES, LANES), F32),
                pltpu.VMEM((rows * SCORES, LANES), F32),
                pltpu.VMEM((field, LANES), F32),
                pltpu.VMEM((field, LANES), F32),
                pltpu.VMEM((field, 2 * LANES), BF16),
                pltpu.VMEM(((ITERS + 1) * 5 * haloed, LANES), F32),
                pltpu.VMEM((ITERS * field, LANES), F32),
                pltpu.VMEM((ITERS * field, LANES), F32),
                pltpu.VMEM((count, LANES), F32),
            ],
        ),
        compiler_params=pltpu.CompilerParams(vmem_limit_bytes=58 * 1024 * 1024),
        name="flag_tiles" if flagged else "res_tiles",
    )(*(lists if flagged else ()), *[kernels] * 5, unary, labels, mask)
    return jnp.transpose(grads, (1, 0, 2)), rows


def on_device(
    flag_kernels,
    flag_unary,
    flag_labels,
    flag_mask,
    dest_list,
    slot_list,
    res_kernels,
    res_unary,
    res_labels,
    res_mask,
):
    ranks = lax.axis_size("length")
    me = lax.axis_index("length").astype(jnp.int32).reshape(1)
    flag_grad, rows = process(
        flag_kernels[0, 0],
        flag_unary[0, 0],
        flag_labels[0, 0],
        flag_mask[0, 0],
        (dest_list[0, 0], slot_list[0, 0], me),
        ranks,
    )
    got = [rows[0]] + [
        lax.ppermute(rows[k], "length", [(i, (i + k) % ranks) for i in range(ranks)])
        for k in range(1, ranks)
    ]
    res_grad, _ = process(
        res_kernels[0, 0], res_unary[0, 0], res_labels[0, 0], res_mask[0, 0], None, ranks
    )
    helper_loss = functools.reduce(jnp.add, got)[:, :RECV]
    return flag_grad[None, None], res_grad[None, None], helper_loss[None]


def solution(mesh):
    tiles = ("groups", "sector", "pair")
    spec = lambda extra: P("length", tiles, *([None] * extra))
    in_specs = tuple(spec(n) for n in (3, 3, 2, 2, 1, 1, 3, 3, 2, 2))
    out_specs = tuple(spec(n) for n in (3, 3, 1))
    return jax.shard_map(
        on_device, mesh=mesh, in_specs=in_specs, out_specs=out_specs, check_vma=False
    )
```

```python
import functools

import jax
import jax.numpy as jnp
from jax import lax
from jax.experimental import pallas as pl
from jax.experimental.pallas import tpu as pltpu
from jax.sharding import PartitionSpec as P

CLASSES = 8
DIFFS = CLASSES - 1
TAPS = 25
TILE = 32
ITERS = 3
RECV = 16
LANES = 128
BLOCKS = 4
PIXELS = TILE * TILE
PAIR = 2 * DIFFS * 8
SCORES = (CLASSES + 2) * 8
F32 = jnp.float32
BF16 = jnp.bfloat16


def dot(left, right):
    return jnp.dot(left, right, preferred_element_type=F32)


def tile_kernel(flagged, width, ranks, *refs):
    if flagged:
        dest_ref, slot_ref, me_ref, *refs = refs
    k_refs, refs = refs[:5], refs[5:]
    u_ref, lab_ref, msk_ref, out_ref, *refs = refs
    if flagged:
        loss_refs, refs = refs[:ranks], refs[ranks:]
    swap, move, down, up, kx, kt, uu, ux, ud, acc, hl, fields, beliefs, grads, sums = refs
    block = pl.program_id(0)
    teams = width // 8
    cuts = BLOCKS // teams
    rows = TILE // cuts
    quads = rows // 4
    field = rows // 2 * PAIR
    haloed = field + 2 * PAIR
    spread = 5 * haloed

    @pl.when(block == 0)
    def _():
        row = lax.broadcasted_iota(jnp.int32, (LANES, LANES), 0)
        lane = lax.broadcasted_iota(jnp.int32, (LANES, LANES), 1)
        same = row % TILE == lane % TILE
        for j in range(BLOCKS):
            for r in range(BLOCKS):
                hit = same & (row // TILE == r) & (lane // TILE == j)
                swap[pl.ds(j * LANES, LANES), pl.ds(r * LANES, LANES)] = jnp.where(
                    hit, 1.0, 0.0
                ).astype(BF16)
        for b in range(5):
            seen = lane % TILE + b - 2
            inside = (seen >= 0) & (seen < TILE)
            cut = lane // TILE % cuts
            for ref, jump in ((move, 0), (down, -TILE), (up, TILE)):
                place = b
                if jump == 0:
                    if b == 2:
                        continue
                    place = b - (b > 2)
                hit = inside & (row == lane + b - 2 + jump)
                if jump:
                    hit = hit & (cut > 0 if jump < 0 else cut < cuts - 1)
                part = jnp.where(hit, 1.0, 0.0).astype(BF16)
                for twice in range(2):
                    ref[pl.ds(twice * LANES, LANES), pl.ds(place * LANES, LANES)] = part
        for ref in (down, up):
            ref[:, pl.ds(5 * LANES, LANES)] = jnp.zeros((2 * LANES, LANES), BF16)
        uu[...] = jnp.zeros_like(uu)
        if flagged:
            sums[...] = jnp.zeros_like(sums)

    if flagged:
        live = jnp.int32(0)
        for j in range(sums.shape[0]):
            live = live + (dest_ref[j] >= 0).astype(jnp.int32)
    else:
        live = jnp.int32(width)

    def kernel_at(t, r):
        return ((r % 4) * quads + r // 4) * TAPS + t

    def field_at(slot, b, r, c):
        place = b * haloed + ((r + 2) // 2) * PAIR + c * 16 + (r % 2) * 8
        return slot * spread + place

    def plain_at(r, c):
        return ((r // 2) * DIFFS + c) * 16 + (r % 2) * 8

    def outside(r):
        return cuts == 1 and not 0 <= r < rows

    def eight(start):
        return pl.ds(pl.multiple_of(start, 8), 8)

    def sixteen(start):
        return pl.ds(pl.multiple_of(start, 16), 16)

    def swapped(left):
        for two in range(BLOCKS // 2):
            got = dot(left, swap[:, pl.ds(two * 2 * LANES, 2 * LANES)])
            yield 2 * two, got[:, :LANES]
            yield 2 * two + 1, got[:, LANES:]

    def bring_kernels():
        for m in range(quads):
            parts = []
            for j in range(BLOCKS):
                team, cut = divmod(j, cuts)
                lanes = pl.ds((m + quads * cut) * LANES, LANES)
                part = jnp.concatenate([ref[:, :, lanes] for ref in k_refs], axis=0)
                part = part.astype(F32)[:, 8 * team : 8 * team + 8]
                parts.append(part.reshape(TAPS * 8, LANES).astype(BF16))
            for r, got in swapped(jnp.concatenate(parts, axis=1)):
                kx[pl.ds((r * quads + m) * TAPS, TAPS), :, :] = got.reshape(
                    TAPS, 8, LANES
                )

    def give_kernels():
        for m in range(quads):
            left = jnp.concatenate(
                [
                    kx[pl.ds((r * quads + m) * TAPS, TAPS), :, :]
                    .reshape(TAPS * 8, LANES)
                    .astype(BF16)
                    for r in range(BLOCKS)
                ],
                axis=1,
            )
            got = {j: part.reshape(TAPS, 8, LANES) for j, part in swapped(left)}
            for cut in range(cuts):
                part = [got[team * cuts + cut] for team in range(teams)]
                lanes = pl.ds((m + quads * cut) * LANES, LANES)
                out_ref[:, :, lanes] = jnp.concatenate(part, axis=1).astype(BF16)

    def emit(slot, pair, c, value):
        fields[sixteen(field_at(slot, 2, 2 * pair, c)), :] = value
        high = value.astype(BF16)
        low = (value - high.astype(F32)).astype(BF16)
        place = pl.ds(plain_at(2 * pair, c), 16)
        hl[place, pl.ds(0, LANES)] = high
        hl[place, pl.ds(LANES, LANES)] = low

    def shift(slot):
        def put(pair, source, matrix, names):
            got = dot(hl[source, :], matrix)
            for n, b in enumerate(names):
                start = field_at(slot, b, 2 * pair, 0)
                fields[pl.ds(pl.multiple_of(start, 16), source.size), :] = got[
                    :, n * LANES : (n + 1) * LANES
                ]

        first, last = pl.ds(0, PAIR), pl.ds(field - PAIR, PAIR)
        for two, names in enumerate(((2, 3), (0, 1), (4,))):
            lanes = pl.ds(names[0] * LANES, 2 * LANES)
            if cuts > 1:
                put(-1, last, down[:, lanes], names)
                put(rows // 2, first, up[:, lanes], names)
            if two == 0:
                put(0, pl.ds(0, field), move[:, pl.ds(0, 2 * LANES)], (0, 1))
            elif two == 1:
                put(0, pl.ds(0, field), move[:, pl.ds(2 * LANES, 2 * LANES)], (3, 4))

    def message(taps_ref, slot, start_ref):
        for quad in range(quads):
            for classes in ((0, 1, 2, 3), (4, 5, 6)):
                totals = {}
                for c in classes:
                    for r in range(4):
                        place = pl.ds(plain_at(4 * quad + r, c), 8)
                        totals[c, r] = None if start_ref is None else start_ref[place, :]
                for b in (2, 0, 1, 3, 4):
                    near = {
                        (c, r): fields[eight(field_at(slot, b, 4 * quad + r - 2, c)), :]
                        for c in classes
                        for r in range(8)
                        if not outside(4 * quad + r - 2)
                    }
                    for a in range(5):
                        for r in range(4):
                            if outside(4 * quad + r + a - 2):
                                continue
                            tap = taps_ref[kernel_at(5 * a + b, 4 * quad + r)]
                            for c in classes:
                                term = tap * near[c, r + a]
                                old = totals[c, r]
                                totals[c, r] = term if old is None else old + term
                for (c, r), total in totals.items():
                    acc[pl.ds(plain_at(4 * quad + r, c), 8), :] = total

    def work():
        for a in range(5):
            for b in range(5):
                for r in range(rows):
                    source = r - (a - 2)
                    turn = b - 2
                    if outside(source):
                        continue
                    if source < 0:
                        source, turn = source + rows, turn + TILE
                    elif source >= rows:
                        source, turn = source - rows, turn - TILE
                    value = kx[kernel_at(5 * a + b, source)]
                    if turn:
                        value = pltpu.roll(value, turn % LANES, 1)
                    kt[kernel_at(5 * (4 - a) + 4 - b, r)] = value

        index = lax.broadcasted_iota(jnp.int32, (8, LANES), 0) + block * width
        for team in range(teams):
            mine = pl.ds(8 * team, 8)
            for s in range(8):
                cut = pl.ds(s * LANES, LANES)
                for i in range(8):
                    uu[team, pl.ds(s * SCORES + i, CLASSES, stride=8), :] = u_ref[
                        8 * team + i, :, cut
                    ].astype(F32)
                target = jnp.where(
                    (index + 8 * team < live) & (msk_ref[mine, cut] == 1),
                    lab_ref[mine, cut],
                    CLASSES,
                )
                uu[team, pl.ds(s * SCORES + 8 * CLASSES, 8), :] = target.astype(F32)
        left = jnp.concatenate(
            [
                jnp.concatenate(
                    [
                        uu[
                            j // cuts, pl.ds((m + quads * (j % cuts)) * SCORES, SCORES), :
                        ].astype(BF16)
                        for j in range(BLOCKS)
                    ],
                    axis=1,
                )
                for m in range(quads)
            ],
            axis=0,
        )
        for r, got in swapped(left):
            ux[pl.ds(r * quads * SCORES, quads * SCORES), :] = got

        def score(r, f):
            return ux[pl.ds(((r % 4) * quads + r // 4) * SCORES + 8 * f, 8), :]

        for r in range(rows):
            last = score(r, CLASSES - 1)
            for c in range(DIFFS):
                value = score(r, c) - last
                ud[pl.ds(plain_at(r, c), 8), :] = value
                acc[pl.ds(plain_at(r, c), 8), :] = value

        def forward(it, carry):
            for pair in range(rows // 2):
                at = lambda c: pl.ds(plain_at(2 * pair, c), 16)
                raised = [jnp.exp(acc[at(c), :]) for c in range(DIFFS)]
                inverse = 1.0 / (functools.reduce(jnp.add, raised) + 1.0)
                for c in range(DIFFS):
                    belief = raised[c] * inverse
                    beliefs[sixteen(it * field + plain_at(2 * pair, c)), :] = belief
                    emit(it, pair, c, belief - inverse)
            shift(it)
            message(kx, it, ud)
            return carry

        lax.fori_loop(0, ITERS, forward, 0)

        lost = jnp.zeros((8, LANES), F32)
        for r in range(rows):
            label = score(r, CLASSES)
            diffs = [acc[pl.ds(plain_at(r, c), 8), :] for c in range(DIFFS)]
            raised = [jnp.exp(d) for d in diffs]
            total = functools.reduce(jnp.add, raised) + 1.0
            inverse = 1.0 / total
            used = label < CLASSES
            chosen = jnp.zeros((8, LANES), F32)
            for c in range(DIFFS):
                hit = label == c
                chosen = jnp.where(hit, diffs[c], chosen)
                slope = raised[c] * inverse - jnp.where(hit, 1.0, 0.0)
                grads[pl.ds((ITERS - 1) * field + plain_at(r, c), 8), :] = jnp.where(
                    used, slope, 0.0
                )
            lost = lost + jnp.where(used, jnp.log(total) - chosen, 0.0)
        if flagged:
            lane = lax.broadcasted_iota(jnp.int32, (8, LANES), 1)
            for team in range(teams):
                one = jnp.where(lane // (cuts * TILE) == team, lost, 0.0)
                one = jnp.sum(one, axis=1, keepdims=True) * (1.0 / TILE)
                sums[eight(block * width + 8 * team), :] = jnp.broadcast_to(one, (8, LANES))

        def backward(step, carry):
            it = ITERS - 1 - step
            for pair in range(rows // 2):
                for c in range(DIFFS):
                    place = plain_at(2 * pair, c)
                    emit(ITERS, pair, c, grads[sixteen(it * field + place), :])
            shift(ITERS)
            message(kt, ITERS, None)
            for pair in range(rows // 2):
                at = lambda c: plain_at(2 * pair, c)
                back = [acc[pl.ds(at(c), 16), :] for c in range(DIFFS)]
                mean = functools.reduce(
                    jnp.add,
                    [
                        back[c] * fields[sixteen(field_at(it, 2, 2 * pair, c)), :]
                        for c in range(DIFFS)
                    ],
                )
                for c in range(DIFFS):
                    belief = beliefs[sixteen(it * field + at(c)), :]
                    grads[sixteen((it - 1) * field + at(c)), :] = belief * (back[c] - mean)
            return carry

        lax.fori_loop(0, ITERS - 1, backward, 0)

        def gather(b, carry):
            for quad in range(quads):
                totals = [[None] * 4 for _ in range(5)]
                for it in range(ITERS):
                    for c in range(DIFFS):
                        near = [
                            None
                            if outside(4 * quad + r - 2)
                            else fields[eight(field_at(it, b, 4 * quad + r - 2, c)), :]
                            for r in range(8)
                        ]
                        for r in range(4):
                            slope = grads[
                                pl.ds(it * field + plain_at(4 * quad + r, c), 8), :
                            ]
                            for a in range(5):
                                if near[r + a] is None:
                                    continue
                                term = slope * near[r + a]
                                old = totals[a][r]
                                totals[a][r] = term if old is None else old + term
                for a in range(5):
                    for r in range(4):
                        total = totals[a][r]
                        if total is None:
                            total = jnp.zeros((8, LANES), F32)
                        kx[kernel_at(5 * a + b, 4 * quad + r)] = total
            return carry

        lax.fori_loop(0, 5, gather, 0)

    @pl.when(live > block * width)
    def _():
        bring_kernels()
        work()
        give_kernels()

    if not flagged:
        return

    @pl.when(live <= block * width)
    def _():
        out_ref[...] = jnp.zeros_like(out_ref)

    @pl.when(block == pl.num_programs(0) - 1)
    def _():
        high = -(-ranks // 8) * 8
        spot = lax.broadcasted_iota(
            jnp.int32, (high, LANES), 0
        ) * LANES + lax.broadcasted_iota(jnp.int32, (high, LANES), 1)
        placed = jnp.zeros((high, LANES), F32)
        for j in range(sums.shape[0]):
            far = dest_ref[j] - me_ref[0]
            far = jnp.where(far < 0, far + ranks, far)
            here = jnp.where(dest_ref[j] >= 0, far * LANES + slot_ref[j], -1)
            placed = jnp.where(spot == here, sums[pl.ds(j, 1), :], placed)
        for k, ref in enumerate(loss_refs):
            ref[...] = placed[k : k + 1, :]


def process(kernels, unary, labels, mask, lists, ranks):
    kernels = jnp.transpose(kernels, (1, 0, 2))
    count = kernels.shape[1]
    flagged = lists is not None
    width = 32 if count % 32 == 0 else 8
    rows = TILE * width // (8 * BLOCKS)
    field = rows // 2 * PAIR
    haloed = field + 2 * PAIR

    out_shape = [jax.ShapeDtypeStruct(kernels.shape, BF16)]
    out_specs = [pl.BlockSpec((TAPS, width, PIXELS), lambda g, *_: (0, g, 0))]
    if flagged:
        out_shape += [jax.ShapeDtypeStruct((1, LANES), F32)] * ranks
        out_specs += [pl.BlockSpec((1, LANES), lambda g, *_: (0, 0))] * ranks
    grads, *rows = pl.pallas_call(
        functools.partial(tile_kernel, flagged, width, ranks),
        out_shape=out_shape,
        grid_spec=pltpu.PrefetchScalarGridSpec(
            num_scalar_prefetch=3 if flagged else 0,
            grid=(count // width,),
            in_specs=[
                *[
                    pl.BlockSpec((5, width, PIXELS), lambda g, *_, a=a: (a, g, 0))
                    for a in range(5)
                ],
                pl.BlockSpec((width, CLASSES, PIXELS), lambda g, *_: (g, 0, 0)),
                pl.BlockSpec((width, PIXELS), lambda g, *_: (g, 0)),
                pl.BlockSpec((width, PIXELS), lambda g, *_: (g, 0)),
            ],
            out_specs=out_specs,
            scratch_shapes=[
                pltpu.VMEM((BLOCKS * LANES, BLOCKS * LANES), BF16),
                pltpu.VMEM((2 * LANES, 4 * LANES), BF16),
                pltpu.VMEM((2 * LANES, 6 * LANES), BF16),
                pltpu.VMEM((2 * LANES, 6 * LANES), BF16),
                pltpu.VMEM((rows * TAPS, 8, LANES), F32),
                pltpu.VMEM((rows * TAPS, 8, LANES), F32),
                pltpu.VMEM((width // 8, 8 * SCORES, LANES), F32),
                pltpu.VMEM((rows * SCORES, LANES), F32),
                pltpu.VMEM((field, LANES), F32),
                pltpu.VMEM((field, LANES), F32),
                pltpu.VMEM((field, 2 * LANES), BF16),
                pltpu.VMEM(((ITERS + 1) * 5 * haloed, LANES), F32),
                pltpu.VMEM((ITERS * field, LANES), F32),
                pltpu.VMEM((ITERS * field, LANES), F32),
                pltpu.VMEM((count, LANES), F32),
            ],
        ),
        compiler_params=pltpu.CompilerParams(vmem_limit_bytes=58 * 1024 * 1024),
        name="flag_tiles" if flagged else "res_tiles",
    )(*(lists if flagged else ()), *[kernels] * 5, unary, labels, mask)
    return jnp.transpose(grads, (1, 0, 2)), rows


def on_device(
    flag_kernels,
    flag_unary,
    flag_labels,
    flag_mask,
    dest_list,
    slot_list,
    res_kernels,
    res_unary,
    res_labels,
    res_mask,
):
    ranks = lax.axis_size("length")
    me = lax.axis_index("length").astype(jnp.int32).reshape(1)
    flag_grad, rows = process(
        flag_kernels[0, 0],
        flag_unary[0, 0],
        flag_labels[0, 0],
        flag_mask[0, 0],
        (dest_list[0, 0], slot_list[0, 0], me),
        ranks,
    )
    got = [rows[0]] + [
        lax.ppermute(rows[k], "length", [(i, (i + k) % ranks) for i in range(ranks)])
        for k in range(1, ranks)
    ]
    res_grad, _ = process(
        res_kernels[0, 0], res_unary[0, 0], res_labels[0, 0], res_mask[0, 0], None, ranks
    )
    helper_loss = functools.reduce(jnp.add, got)[:, :RECV]
    return flag_grad[None, None], res_grad[None, None], helper_loss[None]


def solution(mesh):
    tiles = ("groups", "sector", "pair")
    spec = lambda extra: P("length", tiles, *([None] * extra))
    in_specs = tuple(spec(n) for n in (3, 3, 2, 2, 1, 1, 3, 3, 2, 2))
    out_specs = tuple(spec(n) for n in (3, 3, 1))
    return jax.shard_map(
        on_device, mesh=mesh, in_specs=in_specs, out_specs=out_specs, check_vma=False
    )
```
